256 devices in a mesh: inp: 8 (over z_hi, x), out: 4 (over z_lo), dep: 8 (over y, core).
Axes of the slice: x: 4, y: 4, z: 8 (z_hi: 2, z_lo: 4; z = z_hi * 4 + z_lo), core: 2. Of those that a mesh axis runs over, the one named last changes fastest.
Arguments:
- tokens: bfloat16 [4096, 6144], P(('dep', 'out'), 'inp'), may hold values from -6 to 6
- up_weight: bfloat16 [6144, 24576], P(('inp', 'dep'), 'out'), may hold values from -0.078125 to 0.078125
- hidden_grad: bfloat16 [4096, 24576], P(('dep', 'inp'), 'out'), may hold values from -6 to 6
Outputs:
- hidden: bfloat16 [4096, 24576], P(('dep', 'inp'), 'out')
- input_grad: bfloat16 [4096, 6144], P(('dep', 'out'), 'inp')
- weight_grad: float32 [6144, 24576], P(('inp', 'dep'), 'out')
The draws below stay inside these ranges and needn't reach their ends.
All inputs are finite; a program needn't handle non-finite values.
Results may differ from the reference program's by a relative error of at most 0.022.
Values may be sent and summed in bfloat16 or wider, within the bound.
A program may use at most 128 MiB of HBM per device.

```python
import math
import jax
import jax.numpy as jnp
from jax import lax

D = 6144
FF = 24576
TOK_DEV = 128
TOKENS = 4096
N_OUT = 4
N_DEP = 8


def levels(rng, extent, pieces, low, top_value):
    def one(position, shards_of):
        heights = jax.random.uniform(jax.random.fold_in(jax.random.fold_in(rng, 6), position), (shards_of,), jnp.float32, low / len(pieces), top_value / len(pieces))
        return jnp.repeat(jnp.exp(heights), extent[position] // shards_of).reshape((-1,) + (1,) * (len(extent) - position - 1))

    level = one(*pieces[0])
    for cut in pieces[1:]:
        level = level * one(*cut)
    return level


def scatter_about(own_key, shape, spread, reach, pieces=(), dtype=jnp.bfloat16):
    loudness = levels(own_key, shape, pieces, -0.22, 0.18) if pieces else 1.0
    entries = jax.random.normal(own_key, shape, jnp.float32) * spread * loudness
    return jnp.minimum(jnp.maximum(entries, -reach), reach).astype(dtype)


def setup_inputs(seed: int = 0) -> dict:
    splits = jax.random.split(jax.random.key(seed), 4)
    tokens = scatter_about(splits[0], (TOKENS, D), 1.0, 6.0, ((0, 32), (1, 8)))
    up_weight = scatter_about(splits[1], (D, FF), D ** -0.5, 0.078125, ((0, 64), (1, 4)))
    hidden_grad = scatter_about(splits[2], (TOKENS, FF), 1.0, 6.0, ((0, 64), (1, 4)))
    return {"tokens": tokens, "up_weight": up_weight, "hidden_grad": hidden_grad}


def activation(values):
    return jax.nn.gelu(values, approximate=True)

def reference(tokens, up_weight, hidden_grad):
    pre = jnp.dot(tokens, up_weight, preferred_element_type=jnp.float32)
    hidden = activation(pre).astype(jnp.bfloat16)
    _, pullback = jax.vjp(activation, pre)
    grad_pre = pullback(hidden_grad.astype(jnp.float32))[0].astype(jnp.bfloat16)
    input_grad = lax.dot_general(grad_pre, up_weight, (((1,), (1,)), ((), ())), preferred_element_type=jnp.float32).astype(jnp.bfloat16)
    group_tokens = tokens.reshape(N_DEP, TOK_DEV * N_OUT, D)
    group_grads = grad_pre.reshape(N_DEP, TOK_DEV * N_OUT, FF)

    def add_group(total, pair):
        part = lax.dot_general(pair[0], pair[1], (((0,), (0,)), ((), ())), preferred_element_type=jnp.float32)
        part = lax.optimization_barrier(part.astype(jnp.bfloat16))
        return (total + part.astype(jnp.float32), None)
    total, _ = lax.scan(add_group, jnp.zeros((D, FF), jnp.float32), (group_tokens, group_grads))
    weight_grad = total * (1.0 / math.sqrt(TOKENS))
    return (hidden, input_grad, weight_grad)
```

```python
import functools
import math

import jax
import jax.numpy as jnp
from jax import lax
from jax.experimental import pallas as pl
from jax.experimental.pallas import tpu as pltpu
from jax.sharding import PartitionSpec as P

MESH = pl.DeviceIdType.MESH
BF, F32 = jnp.bfloat16, jnp.float32

NX, NY, NL = 4, 4, 4
C, NC = 256, 12
HALF = C * NC
SUB = 64
ROWS = 96
D = 768

FLOWS = (
    "w_core", "w_up", "w_down", "w_up2", "w_down2", "hg_core",
    "s1_up", "s1_down", "s2_up", "s2_down", "z_pre", "z_grad",
    "g_up", "g_down", "g_up2", "g_down2", "hid_core",
    "q1_up", "q1_down", "q2_up", "q2_down", "wg_core",
)


def act_and_slope(v):
    a, b = math.sqrt(2.0 / math.pi), 0.044715
    sq = v * v
    t = jnp.tanh(a * v * (1.0 + b * sq))
    half = 0.5 * (1.0 + t)
    return v * half, half + (0.5 * a) * v * (1.0 - t * t) * (1.0 + (3.0 * b) * sq)


def kernel(
    tok_in, w_in, hg_in, hid_out, ig_out, wg_out,
    tok, tok_t, wbuf, hgb, part, r1, r2, zs, r3, tot, grad, hs, q, r8, r9, ws, acc, cs, cr,
    lr_send, lr_recv, ll_send, ll_recv, ig_buf,
    f_send, f_recv, w_loc, hg_loc, hid_loc, wg_loc, one_loc,
    t_recv, tc_recv, t_send, tc_send, c_sem, lr_sems, ll_sems,
):
    inp, l, dep = lax.axis_index("inp"), lax.axis_index("out"), lax.axis_index("dep")
    h, x = inp // NX, inp % NX
    y, c = dep // 2, dep % 2
    o = 1 - c

    def dev(h_=h, x_=x, l_=l, y_=y, c_=c):
        return (h_ * NX + x_, l_, y_ * 2 + c_)

    x_up, x_dn, x_far = (x + 1) % NX, (x + 3) % NX, (x + 2) % NX
    y_up, y_dn, y_far = (y + 1) % NY, (y + 3) % NY, (y + 2) % NY
    d_xu, d_xd, d_yu, d_yd = dev(x_=x_up), dev(x_=x_dn), dev(y_=y_up), dev(y_=y_dn)
    d_c, d_z = dev(c_=o), dev(h_=1 - h)
    zpos = h * NL + l
    zu, zd = (zpos + 1) % (2 * NL), (zpos + 2 * NL - 1) % (2 * NL)
    d_zu, d_zd = dev(h_=zu // NL, l_=zu % NL), dev(h_=zd // NL, l_=zd % NL)

    def rc(src, dst, ss, rs, to):
        return pltpu.make_async_remote_copy(
            src_ref=src, dst_ref=dst, send_sem=ss, recv_sem=rs, device_id=to, device_id_type=MESH
        )

    def cols(k, which):
        return pl.ds(pl.multiple_of(which * HALF + k * C, C), C)

    def w_rows(who):
        return pl.ds(pl.multiple_of(who * ROWS, 16), ROWS)

    top, bottom = pl.ds(0, ROWS), pl.ds(ROWS, ROWS)
    table = {
        "w_core": (lambda k: w_in.at[:, cols(k, o)], lambda k: wbuf.at[k, y, w_rows(c)],
                   d_c, lambda k: wbuf.at[k, y, w_rows(o)]),
        "w_up": (lambda k: wbuf.at[k, y], lambda k: wbuf.at[k, y], d_yu, lambda k: wbuf.at[k, y_dn]),
        "w_down": (lambda k: wbuf.at[k, y], lambda k: wbuf.at[k, y], d_yd, lambda k: wbuf.at[k, y_up]),
        "w_up2": (lambda k: wbuf.at[k, y_dn, top], lambda k: wbuf.at[k, y_dn, top],
                  d_yu, lambda k: wbuf.at[k, y_far, top]),
        "w_down2": (lambda k: wbuf.at[k, y_up, bottom], lambda k: wbuf.at[k, y_up, bottom],
                    d_yd, lambda k: wbuf.at[k, y_far, bottom]),
        "hg_core": (lambda k: hg_in.at[:, cols(k, o)], lambda k: hgb.at[k, c],
                    d_c, lambda k: hgb.at[k, o]),
        "s1_up": (lambda k: part.at[k, x_far, 0], lambda k: r1.at[k, 0], d_xu, lambda k: r1.at[k, 0]),
        "s1_down": (lambda k: part.at[k, x_far, 1], lambda k: r1.at[k, 1], d_xd, lambda k: r1.at[k, 1]),
        "s2_up": (lambda k: part.at[k, x_up], lambda k: r2.at[k, 0], d_xu, lambda k: r2.at[k, 0]),
        "s2_down": (lambda k: part.at[k, x_dn], lambda k: r2.at[k, 1], d_xd, lambda k: r2.at[k, 1]),
        "z_pre": (lambda k: zs.at[k], lambda k: r3.at[k], d_z, lambda k: r3.at[k]),
        "z_grad": (lambda k: grad.at[k, x, h], lambda k: grad.at[k, x, h],
                   d_z, lambda k: grad.at[k, x, 1 - h]),
        "g_up": (lambda k: grad.at[k, x], lambda k: grad.at[k, x], d_xu, lambda k: grad.at[k, x_dn]),
        "g_down": (lambda k: grad.at[k, x], lambda k: grad.at[k, x], d_xd, lambda k: grad.at[k, x_up]),
        "g_up2": (lambda k: grad.at[k, x_dn, 0], lambda k: grad.at[k, x_dn, 0],
                  d_xu, lambda k: grad.at[k, x_far, 0]),
        "g_down2": (lambda k: grad.at[k, x_up, 1], lambda k: grad.at[k, x_up, 1],
                    d_xd, lambda k: grad.at[k, x_far, 1]),
        "hid_core": (lambda k: hs.at[k, o], lambda k: hid_out.at[:, cols(k, c)],
                     d_c, lambda k: hid_out.at[:, cols(k, o)]),
        "q1_up": (lambda k: q.at[k, y_far, top], lambda k: r8.at[k, 0], d_yu, lambda k: r8.at[k, 0]),
        "q1_down": (lambda k: q.at[k, y_far, bottom], lambda k: r8.at[k, 1], d_yd, lambda k: r8.at[k, 1]),
        "q2_up": (lambda k: q.at[k, y_up], lambda k: r9.at[k, 0], d_yu, lambda k: r9.at[k, 0]),
        "q2_down": (lambda k: q.at[k, y_dn], lambda k: r9.at[k, 1], d_yd, lambda k: r9.at[k, 1]),
        "wg_core": (lambda k: ws.at[k, o], lambda k: wg_out.at[:, cols(k, c)],
                    d_c, lambda k: wg_out.at[:, cols(k, o)]),
    }

    def desc(name, k):
        src, dst, to, _ = table[name]
        i = FLOWS.index(name)
        return rc(src(k), dst(k), f_send.at[i], f_recv.at[i, k], to)

    def start(name, k):
        @pl.when(k > 0)
        def _():
            desc(name, k - 1).wait_send()

        desc(name, k).start()

    def arrived(name, k):
        src, _, to, got = table[name]
        i = FLOWS.index(name)
        rc(src(k), got(k), f_send.at[i], f_recv.at[i, k], to).wait_recv()

    barrier = pltpu.get_barrier_semaphore()
    friends = (d_xu, d_xd, d_yu, d_yd, d_c, d_z, d_zu, d_zd)
    for d in friends:
        pl.semaphore_signal(barrier, inc=1, device_id=d, device_id_type=MESH)

    def w_local(k):
        return pltpu.make_async_copy(w_in.at[:, cols(k, c)], wbuf.at[k, y, w_rows(c)], w_loc.at[k])

    def hg_local(k):
        return pltpu.make_async_copy(hg_in.at[:, cols(k, c)], hgb.at[k, c], hg_loc.at[k])

    def hid_local(k):
        return pltpu.make_async_copy(hs.at[k, c], hid_out.at[:, cols(k, c)], hid_loc.at[k])

    def wg_local(k):
        return pltpu.make_async_copy(ws.at[k, c], wg_out.at[:, cols(k, c)], wg_loc.at[k])

    def spot(ref, b, g):
        return ref.at[pl.ds(2 * (b % 2), 2), b // 2, g]

    own_tok = pltpu.make_async_copy(tok_in, spot(tok, l, c), one_loc.at[0])
    own_tok.start()

    @pl.loop(0, NC)
    def _(k):
        w_local(k).start()

    pl.semaphore_wait(barrier, len(friends))

    def tok_z(b, way, step):
        return rc(spot(tok, b, c), spot(tok, b, c), t_send.at[way, step], t_recv.at[b],
                  d_zu if way == 0 else d_zd)

    def tok_c(b, g):
        return rc(spot(tok, b, g), spot(tok, b, g), tc_send.at[b], tc_recv.at[b], d_c)

    own_tok.wait()

    def tok_step(step):
        @pl.when((l < NL - 1) & (l >= step))
        def _():
            tok_z(l - step, 0, step).start()

        @pl.when((l > 0) & (l + step < NL))
        def _():
            tok_z(l + step, 1, step).start()

    def tok_take(step):
        @pl.when(l >= step)
        def _():
            tok_z(l - step, 0, step).wait_recv()

        @pl.when(l + step < NL)
        def _():
            tok_z(l + step, 1, step).wait_recv()

    def tok_hand(step):
        @pl.when(l >= step)
        def _():
            tok_c(l - step, c).start()

        @pl.when(l + step < NL)
        def _():
            tok_c(l + step, c).start()

    def w_a(k):
        w_local(k).wait()
        arrived("w_core", k)
        start("w_up", k)
        start("w_down", k)

    def w_b(k):
        arrived("w_up", k)
        start("w_up2", k)
        arrived("w_down", k)
        start("w_down2", k)

    tok_step(0)
    start("w_core", 0)
    start("w_core", 1)
    start("w_core", 2)
    tok_c(l, c).start()
    w_a(0)
    w_a(1)

    @pl.loop(3, NC)
    def _(k):
        start("w_core", k)

    tok_take(1)
    tok_step(1)
    tok_hand(1)
    w_b(0)
    w_a(2)
    tok_take(2)
    tok_step(2)
    tok_hand(2)
    tok_take(3)
    tok_hand(3)
    for b in range(NL):
        tok_c(b, o).wait_recv()
    acc[...] = jnp.zeros_like(acc)

    def pre_stage(k):
        arrived("w_up2", k)
        arrived("w_down2", k)
        hg_local(k).start()
        start("hg_core", k)

        def block(j):
            rows = tok[j].reshape(4 * SUB, D)
            out = jnp.dot(rows, wbuf[k].reshape(D, C), preferred_element_type=F32)
            part[k, j] = out.astype(BF).reshape(2, 2 * SUB, C)

        block(x_far)
        start("s1_up", k)
        start("s1_down", k)

        @pl.loop(0, 3)
        def _(s):
            block((x + 3 + s) % NX)

    def s2_stage(k):
        arrived("s1_up", k)
        part[k, x_up, 0] = (part[k, x_up, 0].astype(F32) + r1[k, 0].astype(F32)).astype(BF)
        start("s2_up", k)
        arrived("s1_down", k)
        part[k, x_dn, 1] = (part[k, x_dn, 1].astype(F32) + r1[k, 1].astype(F32)).astype(BF)
        start("s2_down", k)

    def s3_stage(k):
        arrived("s2_up", k)
        arrived("s2_down", k)

        def total(hh):
            return part[k, x, hh].astype(F32) + r2[k, 0, hh].astype(F32) + r2[k, 1, hh].astype(F32)

        zs[k] = total(1 - h).astype(BF)
        start("z_pre", k)
        tot[k] = total(h)

    def s4_stage(k):
        arrived("z_pre", k)
        hg_local(k).wait()
        arrived("hg_core", k)
        v = tot[k] + r3[k].astype(F32)
        hidden, slope = act_and_slope(v)
        gp = hgb[k].reshape(2 * SUB, C).astype(F32) * slope
        grad[k, x, h] = gp.astype(BF)
        start("z_grad", k)
        hs[k] = hidden.astype(BF).reshape(2, SUB, C)
        hid_local(k).start()
        start("hid_core", k)

    def s5_stage(k):
        arrived("z_grad", k)
        start("g_up", k)
        start("g_down", k)

    def s6_stage(k):
        arrived("g_up", k)
        start("g_up2", k)
        arrived("g_down", k)
        start("g_down2", k)

    def mm_stage(k):
        arrived("g_up2", k)
        arrived("g_down2", k)

        def wblock(j):
            rows = tok_t[pl.ds(pl.multiple_of(j * 2 * ROWS, 64), 2 * ROWS), :]
            out = jnp.dot(rows, grad[k].reshape(16 * SUB, C), preferred_element_type=F32)
            q[k, j] = out.astype(BF)

        wblock(y_far)
        start("q1_up", k)
        start("q1_down", k)

        @pl.loop(0, 3)
        def _(s):
            wblock((y + 3 + s) % NY)

        @pl.loop(0, NX)
        def _(j):
            out = lax.dot_general(
                grad[k, j].reshape(4 * SUB, C), wbuf[k].reshape(D, C), (((1,), (1,)), ((), ())),
                preferred_element_type=F32,
            )
            acc[j] += out

    def q2_stage(k):
        arrived("q1_up", k)
        q[k, y_up, top] = (q[k, y_up, top].astype(F32) + r8[k, 0].astype(F32)).astype(BF)
        start("q2_up", k)
        arrived("q1_down", k)
        q[k, y_dn, bottom] = (q[k, y_dn, bottom].astype(F32) + r8[k, 1].astype(F32)).astype(BF)
        start("q2_down", k)

    def q3_stage(k):
        arrived("q2_up", k)
        arrived("q2_down", k)
        t = q[k, y].astype(F32) + r9[k, 0].astype(F32) + r9[k, 1].astype(F32)
        ws[k] = (t * (1.0 / 64.0)).reshape(2, ROWS, C)
        wg_local(k).start()
        start("wg_core", k)

    def transpose_tokens():
        for j in range(NX):
            tok_t[:, j * 4 * SUB:(j + 1) * 4 * SUB] = tok[j].reshape(4 * SUB, D).T

    def stage(i, off, body):
        k = i - off

        @pl.when((k >= 0) & (k < NC))
        def _():
            body(k)

    @pl.loop(0, NC + 8)
    def _(i):
        stage(i, 4, s5_stage)
        stage(i, 5, s6_stage)
        stage(i, 1, s2_stage)
        stage(i, 0, pre_stage)
        stage(i, 2, s3_stage)
        stage(i, 3, s4_stage)
        stage(i, -1, w_b)
        stage(i, -3, w_a)
        stage(i, 6, mm_stage)
        stage(i, 7, q2_stage)
        stage(i, 8, q3_stage)
        pl.when(i == 1)(transpose_tokens)

    sums = acc.reshape(NX, 2, 2, SUB, D)
    for hh in range(2):
        cs[:, hh] = sums[:, hh, o].astype(BF)
    to_core = rc(cs, cr, c_sem.at[0], c_sem.at[1], d_c)
    to_core.start()
    to_core.wait_recv()

    def mine(b):
        s = pl.ds(2 * (b % 2), 2)
        return sums[s, b // 2, c] + cr[s, b // 2].astype(F32)

    def line(b, way):
        if way == 0:
            return rc(lr_send.at[b], lr_recv.at[b], lr_sems.at[0, b], lr_sems.at[1, b], d_zu)
        return rc(ll_send.at[b], ll_recv.at[b], ll_sems.at[0, b], ll_sems.at[1, b], d_zd)

    def go_right(b):
        @pl.when(l == 0)
        def _():
            lr_send[b] = mine(b).astype(BF)

        @pl.when((l > 0) & (l < b))
        def _():
            line(b, 0).wait_recv()
            lr_send[b] = (mine(b) + lr_recv[b].astype(F32)).astype(BF)

        @pl.when(l < b)
        def _():
            line(b, 0).start()

    def go_left(b):
        @pl.when(l == NL - 1)
        def _():
            ll_send[b] = mine(b).astype(BF)

        @pl.when((l < NL - 1) & (l > b))
        def _():
            line(b, 1).wait_recv()
            ll_send[b] = (mine(b) + ll_recv[b].astype(F32)).astype(BF)

        @pl.when(l > b)
        def _():
            line(b, 1).start()

    for b in range(NL - 1):
        go_right(NL - 1 - b)
        go_left(b)

    def finish(b):
        @pl.when(l == b)
        def _():
            t = mine(b)
            if b > 0:
                line(b, 0).wait_recv()
                t = t + lr_recv[b].astype(F32)
            if b < NL - 1:
                line(b, 1).wait_recv()
                t = t + ll_recv[b].astype(F32)
            ig_buf[...] = t.astype(BF)

    for b in range(NL):
        finish(b)
    out_ig = pltpu.make_async_copy(ig_buf, ig_out, one_loc.at[0])
    out_ig.start()

    last = NC - 1
    for name in FLOWS:
        desc(name, last).wait_send()

    @pl.loop(0, NC)
    def _(k):
        arrived("hid_core", k)
        arrived("wg_core", k)
        hid_local(k).wait()
        wg_local(k).wait()

    for step in range(NL - 1):
        @pl.when((l < NL - 1) & (l >= step))
        def _():
            tok_z(l - step, 0, step).wait_send()

        @pl.when((l > 0) & (l + step < NL))
        def _():
            tok_z(l + step, 1, step).wait_send()

    for b in range(NL):
        tok_c(b, c).wait_send()
    to_core.wait_send()
    for b in range(1, NL):
        @pl.when(l < b)
        def _():
            line(b, 0).wait_send()

    for b in range(NL - 1):
        @pl.when(l > b)
        def _():
            line(b, 1).wait_send()

    out_ig.wait()


def on_device(tokens, up_weight, hidden_grad):
    hbm = pl.BlockSpec(memory_space=pl.ANY)
    nf = len(FLOWS)
    dma = pltpu.SemaphoreType.DMA
    hidden, ig, wg = pl.pallas_call(
        kernel,
        out_shape=(
            jax.ShapeDtypeStruct((SUB, 2 * HALF), BF),
            jax.ShapeDtypeStruct((2, SUB, D), BF),
            jax.ShapeDtypeStruct((ROWS, 2 * HALF), F32),
        ),
        in_specs=[hbm] * 3,
        out_specs=[hbm] * 3,
        scratch_shapes=[
            pltpu.VMEM((NX, 2, 2, SUB, D), BF),
            pltpu.VMEM((D, 16 * SUB), BF),
            pltpu.VMEM((NC, NY, 2 * ROWS, C), BF),
            pltpu.VMEM((NC, 2, SUB, C), BF),
            pltpu.VMEM((NC, NX, 2, 2 * SUB, C), BF),
            pltpu.VMEM((NC, 2, 2 * SUB, C), BF),
            pltpu.VMEM((NC, 2, 2, 2 * SUB, C), BF),
            pltpu.VMEM((NC, 2 * SUB, C), BF),
            pltpu.VMEM((NC, 2 * SUB, C), BF),
            pltpu.VMEM((NC, 2 * SUB, C), F32),
            pltpu.VMEM((NC, NX, 2, 2 * SUB, C), BF),
            pltpu.VMEM((NC, 2, SUB, C), BF),
            pltpu.VMEM((NC, NY, 2 * ROWS, C), BF),
            pltpu.VMEM((NC, 2, ROWS, C), BF),
            pltpu.VMEM((NC, 2, 2 * ROWS, C), BF),
            pltpu.VMEM((NC, 2, ROWS, C), F32),
            pltpu.VMEM((NX, 4 * SUB, D), F32),
            pltpu.VMEM((NX, 2, SUB, D), BF),
            pltpu.VMEM((NX, 2, SUB, D), BF),
            pltpu.VMEM((NL, 2, SUB, D), BF),
            pltpu.VMEM((NL, 2, SUB, D), BF),
            pltpu.VMEM((NL, 2, SUB, D), BF),
            pltpu.VMEM((NL, 2, SUB, D), BF),
            pltpu.VMEM((2, SUB, D), BF),
            dma((nf,)), dma((nf, NC)),
            dma((NC,)), dma((NC,)), dma((NC,)), dma((NC,)), dma((1,)),
            dma((NL,)), dma((NL,)), dma((2, NL)), dma((NL,)), dma((2,)),
            dma((2, NL)), dma((2, NL)),
        ],
        name="block",
        compiler_params=pltpu.CompilerParams(
            collective_id=0, has_side_effects=True, vmem_limit_bytes=62 << 20
        ),
    )(tokens.reshape(2, SUB, D), up_weight, hidden_grad)
    return hidden, ig.reshape(2 * SUB, D), wg


def solution(mesh):
    placed = (P(("dep", "out"), "inp"), P(("inp", "dep"), "out"), P(("dep", "inp"), "out"))
    return jax.shard_map(
        on_device,
        mesh=mesh,
        in_specs=placed,
        out_specs=(P(("dep", "inp"), "out"), P(("dep", "out"), "inp"), P(("inp", "dep"), "out")),
        check_vma=False,
    )
```

```python
import functools
import math

import jax
import jax.numpy as jnp
from jax import lax
from jax.experimental import pallas as pl
from jax.experimental.pallas import tpu as pltpu
from jax.sharding import PartitionSpec as P

MESH = pl.DeviceIdType.MESH
BF, F32 = jnp.bfloat16, jnp.float32

NX, NY, NL = 4, 4, 4
C, NC = 256, 12
HALF = C * NC
SUB = 64
ROWS = 96
D = 768
TOKENS = 4096
PARTS = 6

FLOWS = (
    "w_core", "w_up", "w_down", "w_up2", "w_down2", "hg_core",
    "s1_up", "s1_down", "s2_up", "s2_down", "z_pre", "z_grad",
    "g_up", "g_down", "g_up2", "g_down2", "hid_core",
    "q1_up", "q1_down", "q2_up", "q2_down", "wg_core",
)
SLOTS = 4
ORDER = (
    ("s6", 10), ("s5", 8), ("pre2", 2), ("pre1", 0), ("pre3", 4), ("s4", 6),
    ("w_b", -2), ("w_a", -3), ("s7", 12), ("q2", 14), ("q3", 16),
)


def act_and_slope(v):
    a, b = math.sqrt(2.0 / math.pi), 0.044715
    sq = v * v
    t = jnp.tanh(a * v * (1.0 + b * sq))
    half = 0.5 * (1.0 + t)
    return v * half, half + (0.5 * a) * v * (1.0 - t * t) * (1.0 + (3.0 * b) * sq)


def kernel(
    tok_in, w_in, hg_in, hid_out, ig_out, wg_out,
    tok, wbuf, hgb, s1, r1, s2, r2, zs, r3, tot, grad, hs, q, r8, r9, ws, acc, cs, cr,
    lr_send, lr_recv, ll_send, ll_recv, ig_buf, ig_bf,
    f_send, f_recv, w_loc, hg_loc, hid_loc, wg_loc, one_loc,
    t_recv, t_send, tc_recv, tc_send, c_send, c_recv, lr_ss, lr_rs, ll_ss, ll_rs,
):
    inp, l, dep = lax.axis_index("inp"), lax.axis_index("out"), lax.axis_index("dep")
    h, x = inp // NX, inp % NX
    y, c = dep // 2, dep % 2
    o = 1 - c

    def dev(h_=h, x_=x, l_=l, y_=y, c_=c):
        return (h_ * NX + x_, l_, y_ * 2 + c_)

    x_up, x_dn, x_far = (x + 1) % NX, (x + 3) % NX, (x + 2) % NX
    y_up, y_dn, y_far = (y + 1) % NY, (y + 3) % NY, (y + 2) % NY
    d_xu, d_xd, d_yu, d_yd = dev(x_=x_up), dev(x_=x_dn), dev(y_=y_up), dev(y_=y_dn)
    d_c, d_z = dev(c_=o), dev(h_=1 - h)
    zpos = h * NL + l
    zu, zd = (zpos + 1) % (2 * NL), (zpos + 2 * NL - 1) % (2 * NL)
    d_zu, d_zd = dev(h_=zu // NL, l_=zu % NL), dev(h_=zd // NL, l_=zd % NL)

    def rc(src, dst, ss, rs, to):
        return pltpu.make_async_remote_copy(
            src_ref=src, dst_ref=dst, send_sem=ss, recv_sem=rs, device_id=to, device_id_type=MESH
        )

    def cols(k, which):
        return pl.ds(pl.multiple_of(which * HALF + k * C, C), C)

    def w_rows(who):
        return pl.ds(pl.multiple_of(who * ROWS, 16), ROWS)

    top, bottom = pl.ds(0, ROWS), pl.ds(ROWS, ROWS)
    table = {
        "w_core": (lambda k: w_in.at[:, cols(k, o)], lambda k: wbuf.at[k, y, w_rows(c)],
                   d_c, lambda k: wbuf.at[k, y, w_rows(o)]),
        "w_up": (lambda k: wbuf.at[k, y], lambda k: wbuf.at[k, y], d_yu, lambda k: wbuf.at[k, y_dn]),
        "w_down": (lambda k: wbuf.at[k, y], lambda k: wbuf.at[k, y], d_yd, lambda k: wbuf.at[k, y_up]),
        "w_up2": (lambda k: wbuf.at[k, y_dn, top], lambda k: wbuf.at[k, y_dn, top],
                  d_yu, lambda k: wbuf.at[k, y_far, top]),
        "w_down2": (lambda k: wbuf.at[k, y_up, bottom], lambda k: wbuf.at[k, y_up, bottom],
                    d_yd, lambda k: wbuf.at[k, y_far, bottom]),
        "hg_core": (lambda k: hg_in.at[:, cols(k, o)], lambda k: hgb.at[k, c],
                    d_c, lambda k: hgb.at[k, o]),
        "s1_up": (lambda k: s1.at[k, 0], lambda k: r1.at[k, 0], d_xu, lambda k: r1.at[k, 0]),
        "s1_down": (lambda k: s1.at[k, 1], lambda k: r1.at[k, 1], d_xd, lambda k: r1.at[k, 1]),
        "s2_up": (lambda k: s2.at[k, 0], lambda k: r2.at[k, 0], d_xu, lambda k: r2.at[k, 0]),
        "s2_down": (lambda k: s2.at[k, 1], lambda k: r2.at[k, 1], d_xd, lambda k: r2.at[k, 1]),
        "z_pre": (lambda k: zs.at[k], lambda k: r3.at[k], d_z, lambda k: r3.at[k]),
        "z_grad": (lambda k: grad.at[k, x, h], lambda k: grad.at[k, x, h],
                   d_z, lambda k: grad.at[k, x, 1 - h]),
        "g_up": (lambda k: grad.at[k, x], lambda k: grad.at[k, x], d_xu, lambda k: grad.at[k, x_dn]),
        "g_down": (lambda k: grad.at[k, x], lambda k: grad.at[k, x], d_xd, lambda k: grad.at[k, x_up]),
        "g_up2": (lambda k: grad.at[k, x_dn, 0], lambda k: grad.at[k, x_dn, 0],
                  d_xu, lambda k: grad.at[k, x_far, 0]),
        "g_down2": (lambda k: grad.at[k, x_up, 1], lambda k: grad.at[k, x_up, 1],
                    d_xd, lambda k: grad.at[k, x_far, 1]),
        "hid_core": (lambda k: hs.at[k, o], lambda k: hid_out.at[:, cols(k, c)],
                     d_c, lambda k: hid_out.at[:, cols(k, o)]),
        "q1_up": (lambda k: q.at[k, y_far, top], lambda k: r8.at[k, 0], d_yu, lambda k: r8.at[k, 0]),
        "q1_down": (lambda k: q.at[k, y_far, bottom], lambda k: r8.at[k, 1], d_yd, lambda k: r8.at[k, 1]),
        "q2_up": (lambda k: q.at[k, y_up], lambda k: r9.at[k, 0], d_yu, lambda k: r9.at[k, 0]),
        "q2_down": (lambda k: q.at[k, y_dn], lambda k: r9.at[k, 1], d_yd, lambda k: r9.at[k, 1]),
        "wg_core": (lambda k: ws.at[k, o], lambda k: wg_out.at[:, cols(k, c)],
                    d_c, lambda k: wg_out.at[:, cols(k, o)]),
    }

    def desc(name, k):
        src, dst, to, _ = table[name]
        i = FLOWS.index(name)
        return rc(src(k), dst(k), f_send.at[i, k % SLOTS], f_recv.at[i, k], to)

    def when(cond, body):
        if isinstance(cond, bool):
            if cond:
                body()
        else:
            pl.when(cond)(body)

    def start(name, k):
        when(k >= SLOTS, lambda: desc(name, k - SLOTS).wait_send())
        desc(name, k).start()

    def arrived(name, k):
        src, _, to, got = table[name]
        i = FLOWS.index(name)
        rc(src(k), got(k), f_send.at[i, k % SLOTS], f_recv.at[i, k], to).wait_recv()

    barrier = pltpu.get_barrier_semaphore()
    friends = (d_xu, d_xd, d_yu, d_yd, d_c, d_z, d_zu, d_zd)
    for d in friends:
        pl.semaphore_signal(barrier, inc=1, device_id=d, device_id_type=MESH)

    def w_local(k):
        return pltpu.make_async_copy(w_in.at[:, cols(k, c)], wbuf.at[k, y, w_rows(c)], w_loc.at[k])

    def hg_local(k):
        return pltpu.make_async_copy(hg_in.at[:, cols(k, c)], hgb.at[k, c], hg_loc.at[k])

    def hid_local(k):
        return pltpu.make_async_copy(hs.at[k, c], hid_out.at[:, cols(k, c)], hid_loc.at[k])

    def wg_local(k):
        return pltpu.make_async_copy(ws.at[k, c], wg_out.at[:, cols(k, c)], wg_loc.at[k])

    def spot(ref, b, g):
        return ref.at[pl.ds(2 * (b % 2), 2), b // 2, g]

    own_tok = pltpu.make_async_copy(tok_in, spot(tok, l, c), one_loc.at[0])
    own_tok.start()

    @pl.loop(0, NC)
    def _(k):
        w_local(k).start()

    pl.semaphore_wait(barrier, len(friends))

    def tok_z(j, hh, way):
        return rc(tok.at[j, hh, c], tok.at[j, hh, c], t_send.at[way, j, hh], t_recv.at[j, hh],
                  d_zu if way == 0 else d_zd)

    def tok_c(j, hh, g):
        return rc(tok.at[j, hh, g], tok.at[j, hh, g], tc_send.at[j, hh], tc_recv.at[j, hh], d_c)

    def tok_step(j, step):
        for hh in range(2):
            b = j // 2 + 2 * hh

            def right():
                tok_z(j, hh, 0).start()

            def left():
                tok_z(j, hh, 1).start()

            def pass_on(ways):
                if step > 0:
                    tok_z(j, hh, 0).wait_recv()
                for cond, send in ways:
                    pl.when(cond)(send)
                tok_c(j, hh, c).start()

            if step == 0:
                pl.when(l == b)(lambda: pass_on(((l < NL - 1, right), (l > 0, left))))
            else:
                pl.when(l == b + step)(lambda: pass_on(((l < NL - 1, right),)))
                pl.when(l == b - step)(lambda: pass_on(((l > 0, left),)))

    def tok_ready(j):
        for hh in range(2):
            tok_c(j, hh, 1 - c).wait_recv()

    def dot_pre(j, k):
        rows = tok[j].reshape(4 * SUB, D)
        return jnp.dot(rows, wbuf[k].reshape(D, C), preferred_element_type=F32)

    def add_input(j, k):
        acc[j] += lax.dot_general(
            grad[k, j].reshape(4 * SUB, C), wbuf[k].reshape(D, C), (((1,), (1,)), ((), ())),
            preferred_element_type=F32,
        )

    def w_a(k):
        w_local(k).wait()
        arrived("w_core", k)
        start("w_up", k)
        start("w_down", k)

    def w_b(k):
        arrived("w_up", k)
        start("w_up2", k)
        arrived("w_down", k)
        start("w_down2", k)

    def pre1(k):
        arrived("w_up2", k)
        arrived("w_down2", k)
        s1[k] = dot_pre(x_far, k).astype(BF).reshape(2, 2 * SUB, C)
        start("s1_up", k)
        start("s1_down", k)
        hg_local(k).start()
        start("hg_core", k)

    def pre2(k):
        out = dot_pre(x_up, k).reshape(2, 2 * SUB, C)
        arrived("s1_up", k)
        s2[k, 0, 0] = (out[0] + r1[k, 0].astype(F32)).astype(BF)
        s2[k, 0, 1] = out[1].astype(BF)
        start("s2_up", k)
        out = dot_pre(x_dn, k).reshape(2, 2 * SUB, C)
        arrived("s1_down", k)
        s2[k, 1, 0] = out[0].astype(BF)
        s2[k, 1, 1] = (out[1] + r1[k, 1].astype(F32)).astype(BF)
        start("s2_down", k)

    def pre3(k):
        out = dot_pre(x, k).reshape(2, 2 * SUB, C)
        arrived("s2_up", k)
        arrived("s2_down", k)
        tot[k] = out + r2[k, 0].astype(F32) + r2[k, 1].astype(F32)
        zs[k] = tot[k, 1 - h].astype(BF)
        start("z_pre", k)

    def s4(k):
        hg_local(k).wait()
        arrived("hg_core", k)
        arrived("z_pre", k)
        v = tot[k, h] + r3[k].astype(F32)
        hidden, slope = act_and_slope(v)
        gp = hgb[k].reshape(2 * SUB, C).astype(F32) * slope
        grad[k, x, h] = gp.astype(BF)
        start("z_grad", k)
        hs[k] = hidden.astype(BF).reshape(2, SUB, C)
        hid_local(k).start()
        start("hid_core", k)

    def s5(k):
        arrived("z_grad", k)
        start("g_up", k)
        start("g_down", k)
        add_input(x, k)

    def s6(k):
        arrived("g_up", k)
        start("g_up2", k)
        arrived("g_down", k)
        start("g_down2", k)
        add_input(x_up, k)
        add_input(x_dn, k)

    def s7(k):
        arrived("g_up2", k)
        arrived("g_down2", k)
        add_input(x_far, k)
        out = lax.dot_general(
            tok[...].reshape(16 * SUB, D), grad[k].reshape(16 * SUB, C), (((0,), (0,)), ((), ())),
            preferred_element_type=F32,
        )
        q[k] = out.astype(BF).reshape(NY, 2 * ROWS, C)
        start("q1_up", k)
        start("q1_down", k)

    def q2(k):
        arrived("q1_up", k)
        q[k, y_up, top] = (q[k, y_up, top].astype(F32) + r8[k, 0].astype(F32)).astype(BF)
        start("q2_up", k)
        arrived("q1_down", k)
        q[k, y_dn, bottom] = (q[k, y_dn, bottom].astype(F32) + r8[k, 1].astype(F32)).astype(BF)
        start("q2_down", k)

    def q3(k):
        arrived("q2_up", k)
        arrived("q2_down", k)
        t = q[k, y].astype(F32) + r9[k, 0].astype(F32) + r9[k, 1].astype(F32)
        ws[k] = t.astype(BF).reshape(2, ROWS, C)
        wg_local(k).start()
        start("wg_core", k)

    stages = dict(w_a=w_a, w_b=w_b, pre1=pre1, pre2=pre2, pre3=pre3, s4=s4, s5=s5, s6=s6, s7=s7,
                  q2=q2, q3=q3)
    offset = dict(ORDER)

    def run(i, after=None):
        for name, off in ORDER:
            k = i - off
            body = stages[name]
            if isinstance(k, int):
                if 0 <= k < NC:
                    body(k)
                    if after is not None and k == NC - 1 and name in after:
                        after[name]()
            else:
                pl.when((k >= 0) & (k < NC))(functools.partial(body, k))

    sums = acc.reshape(NX, 2, 2, SUB, D)

    def to_core(j):
        return rc(cs.at[j], cr.at[j], c_send.at[j], c_recv.at[j], d_c)

    def ig_give(j):
        for hh in range(2):
            cs[j, hh] = sums[j, hh, o].astype(BF)
        to_core(j).start()

    def mine(j, hh):
        return sums[j, hh, c] + cr[j, hh].astype(F32)

    def line(j, hh, way):
        if way == 0:
            return rc(lr_send.at[j, hh], lr_recv.at[j, hh], lr_ss.at[j, hh], lr_rs.at[j, hh], d_zu)
        return rc(ll_send.at[j, hh], ll_recv.at[j, hh], ll_ss.at[j, hh], ll_rs.at[j, hh], d_zd)

    def ig_step(j, step):
        if step == 0:
            to_core(j).wait_recv()
        for hh in range(2):
            b = j // 2 + 2 * hh

            def move(way):
                out_buf, in_buf = (lr_send, lr_recv) if way == 0 else (ll_send, ll_recv)
                t = mine(j, hh)
                if step > 0:
                    line(j, hh, way).wait_recv()
                    t = t + in_buf[j, hh].astype(F32)
                out_buf[j, hh] = t.astype(BF)
                line(j, hh, way).start()

            pl.when((l == step) & (b > l))(functools.partial(move, 0))
            pl.when((l == NL - 1 - step) & (b < l))(functools.partial(move, 1))

    def ig_end(j):
        for hh in range(2):
            b = j // 2 + 2 * hh

            @pl.when(l == b)
            def _():
                spot_ = j % 2
                ig_buf[spot_] = mine(j, hh)

                @pl.when(l > 0)
                def _():
                    line(j, hh, 0).wait_recv()
                    ig_buf[spot_] += lr_recv[j, hh].astype(F32)

                @pl.when(l < NL - 1)
                def _():
                    line(j, hh, 1).wait_recv()
                    ig_buf[spot_] += ll_recv[j, hh].astype(F32)

                ig_bf[spot_] = ig_buf[spot_].astype(BF)

    own_tok.wait()
    start("w_core", 0)
    tok_step(x_far, 0)
    w_a(0)
    for k in range(1, SLOTS):
        start("w_core", k)
    tok_step(x_up, 0)
    w_a(1)
    tok_step(x_far, 1)
    tok_step(x_dn, 0)
    w_b(0)
    tok_step(x_up, 1)
    tok_step(x_far, 2)
    tok_step(x, 0)

    @pl.loop(SLOTS, NC)
    def _(k):
        start("w_core", k)

    acc[...] = jnp.zeros_like(acc)
    tok_step(x_dn, 1)
    tok_step(x_up, 2)
    w_b(1)
    w_a(2)
    tok_step(x_far, 3)
    tok_ready(x_far)
    run(0)
    tok_step(x, 1)
    tok_step(x_dn, 2)
    tok_step(x_up, 3)
    run(1)
    tok_step(x, 2)
    tok_step(x_dn, 3)
    tok_step(x, 3)
    tok_ready(x_up)
    tok_ready(x_dn)
    tok_ready(x)

    first_end = offset["s5"] + NC - 1
    pl.loop(2, first_end)(run)

    def after_s6():
        ig_step(x, 0)
        ig_give(x_up)
        ig_give(x_dn)
        ig_step(x, 1)

    def after_s7():
        ig_give(x_far)
        ig_step(x_up, 0)
        ig_step(x_dn, 0)
        ig_step(x, 2)
        ig_step(x_far, 0)
        ig_step(x_up, 1)
        ig_step(x_dn, 1)

    def after_q2():
        ig_step(x_far, 1)
        ig_step(x_up, 2)
        ig_step(x_dn, 2)
        ig_step(x_far, 2)

    after = {"s5": lambda: ig_give(x), "s6": after_s6, "s7": after_s7, "q2": after_q2}
    for i in range(first_end, offset["q3"] + NC):
        run(i, after)
    for j in (x, x_up, x_dn, x_far):
        ig_end(j)
    out_ig = pltpu.make_async_copy(ig_bf, ig_out, one_loc.at[0])
    out_ig.start()

    for name in FLOWS:
        for k in range(NC - SLOTS, NC):
            desc(name, k).wait_send()

    @pl.loop(0, NC)
    def _(k):
        arrived("hid_core", k)
        arrived("wg_core", k)
        hid_local(k).wait()
        wg_local(k).wait()

    for j in range(NX):
        for hh in range(2):
            b = j // 2 + 2 * hh
            pl.when((l >= b) & (l < NL - 1))(lambda: tok_z(j, hh, 0).wait_send())
            pl.when((l <= b) & (l > 0))(lambda: tok_z(j, hh, 1).wait_send())
            tok_c(j, hh, c).wait_send()
            pl.when(l < b)(lambda: line(j, hh, 0).wait_send())
            pl.when(l > b)(lambda: line(j, hh, 1).wait_send())
        to_core(j).wait_send()
    out_ig.wait()


def finish_kernel(hid_in, ig_in, wg_in, hid_out, ig_out, wg_out, hid, ig, half, full, in_sems, out_sems):
    rows = ROWS // PARTS

    def load(p):
        return pltpu.make_async_copy(wg_in.at[pl.ds(p * rows, rows)], half.at[p], in_sems.at[p])

    def store(p):
        return pltpu.make_async_copy(full.at[p], wg_out.at[pl.ds(p * rows, rows)], out_sems.at[p])

    through = (
        (pltpu.make_async_copy(hid_in, hid, in_sems.at[PARTS]),
         pltpu.make_async_copy(hid, hid_out, out_sems.at[PARTS])),
        (pltpu.make_async_copy(ig_in, ig, in_sems.at[PARTS + 1]),
         pltpu.make_async_copy(ig, ig_out, out_sems.at[PARTS + 1])),
    )
    for p in range(PARTS):
        load(p).start()
    for come, _ in through:
        come.start()
    for p in range(PARTS):
        load(p).wait()
        full[p] = half[p].astype(F32) * (1.0 / math.sqrt(TOKENS))
        store(p).start()
    for come, go in through:
        come.wait()
        go.start()
    for p in range(PARTS):
        store(p).wait()
    for _, go in through:
        go.wait()


def on_device(tokens, up_weight, hidden_grad):
    hbm = pl.BlockSpec(memory_space=pl.ANY)
    nf = len(FLOWS)
    dma = pltpu.SemaphoreType.DMA
    hidden, ig, wg = pl.pallas_call(
        kernel,
        out_shape=(
            jax.ShapeDtypeStruct((SUB, 2 * HALF), BF),
            jax.ShapeDtypeStruct((2, SUB, D), BF),
            jax.ShapeDtypeStruct((ROWS, 2 * HALF), BF),
        ),
        in_specs=[hbm] * 3,
        out_specs=[hbm] * 3,
        scratch_shapes=[
            pltpu.VMEM((NX, 2, 2, SUB, D), BF),
            pltpu.VMEM((NC, NY, 2 * ROWS, C), BF),
            pltpu.VMEM((NC, 2, SUB, C), BF),
            pltpu.VMEM((NC, 2, 2 * SUB, C), BF),
            pltpu.VMEM((NC, 2, 2 * SUB, C), BF),
            pltpu.VMEM((NC, 2, 2, 2 * SUB, C), BF),
            pltpu.VMEM((NC, 2, 2, 2 * SUB, C), BF),
            pltpu.VMEM((NC, 2 * SUB, C), BF),
            pltpu.VMEM((NC, 2 * SUB, C), BF),
            pltpu.VMEM((NC, 2, 2 * SUB, C), F32),
            pltpu.VMEM((NC, NX, 2, 2 * SUB, C), BF),
            pltpu.VMEM((NC, 2, SUB, C), BF),
            pltpu.VMEM((NC, NY, 2 * ROWS, C), BF),
            pltpu.VMEM((NC, 2, ROWS, C), BF),
            pltpu.VMEM((NC, 2, 2 * ROWS, C), BF),
            pltpu.VMEM((NC, 2, ROWS, C), BF),
            pltpu.VMEM((NX, 4 * SUB, D), F32),
            pltpu.VMEM((NX, 2, SUB, D), BF),
            pltpu.VMEM((NX, 2, SUB, D), BF),
            pltpu.VMEM((NX, 2, SUB, D), BF),
            pltpu.VMEM((NX, 2, SUB, D), BF),
            pltpu.VMEM((NX, 2, SUB, D), BF),
            pltpu.VMEM((NX, 2, SUB, D), BF),
            pltpu.VMEM((2, SUB, D), F32),
            pltpu.VMEM((2, SUB, D), BF),
            dma((nf, SLOTS)), dma((nf, NC)),
            dma((NC,)), dma((NC,)), dma((NC,)), dma((NC,)), dma((1,)),
            dma((NX, 2)), dma((2, NX, 2)), dma((NX, 2)), dma((NX, 2)), dma((NX,)), dma((NX,)),
            dma((NX, 2)), dma((NX, 2)), dma((NX, 2)), dma((NX, 2)),
        ],
        name="block",
        compiler_params=pltpu.CompilerParams(
            collective_id=0, has_side_effects=True, vmem_limit_bytes=62 << 20
        ),
    )(tokens.reshape(2, SUB, D), up_weight, hidden_grad)
    hidden, ig, wg = pl.pallas_call(
        finish_kernel,
        out_shape=(
            jax.ShapeDtypeStruct((SUB, 2 * HALF), BF),
            jax.ShapeDtypeStruct((2, SUB, D), BF),
            jax.ShapeDtypeStruct((ROWS, 2 * HALF), F32),
        ),
        in_specs=[hbm] * 3,
        out_specs=[hbm] * 3,
        scratch_shapes=[
            pltpu.VMEM((SUB, 2 * HALF), BF),
            pltpu.VMEM((2, SUB, D), BF),
            pltpu.VMEM((PARTS, ROWS // PARTS, 2 * HALF), BF),
            pltpu.VMEM((PARTS, ROWS // PARTS, 2 * HALF), F32),
            dma((PARTS + 2,)), dma((PARTS + 2,)),
        ],
        name="finish",
        compiler_params=pltpu.CompilerParams(vmem_limit_bytes=62 << 20),
    )(hidden, ig, wg)
    return hidden, ig.reshape(2 * SUB, D), wg


def solution(mesh):
    placed = (P(("dep", "out"), "inp"), P(("inp", "dep"), "out"), P(("dep", "inp"), "out"))
    return jax.shard_map(
        on_device,
        mesh=mesh,
        in_specs=placed,
        out_specs=(P(("dep", "inp"), "out"), P(("dep", "out"), "inp"), P(("inp", "dep"), "out")),
        check_vma=False,
    )
```

```python
import functools
import math

import jax
import jax.numpy as jnp
from jax import lax
from jax.experimental import pallas as pl
from jax.experimental.pallas import tpu as pltpu
from jax.sharding import PartitionSpec as P

MESH = pl.DeviceIdType.MESH
BF, F32 = jnp.bfloat16, jnp.float32

NX, NY, NL = 4, 4, 4
C, NC = 256, 12
HALF = C * NC
SUB = 64
ROWS = 96
D = 768
TOKENS = 4096
PARTS = 6

FLOWS = (
    "w_core", "w_up", "w_down", "w_up2", "w_down2", "hg_core",
    "s1_up", "s1_down", "s2_up", "s2_down", "z_pre", "z_grad",
    "g_up", "g_down", "g_up2", "g_down2", "hid_core",
    "q1_up", "q1_down", "q2_up", "q2_down", "wg_core",
)
SLOTS = 4
ORDER = (
    ("s6", 12), ("s5", 10), ("pre2", 2), ("pre1", 0), ("pre3", 4), ("s4", 7),
    ("w_b", -2), ("w_a", -3), ("s7", 14), ("q2", 16), ("q3", 18),
)


def act_and_slope(v):
    a, b = math.sqrt(2.0 / math.pi), 0.044715
    sq = v * v
    t = jnp.tanh(a * v * (1.0 + b * sq))
    half = 0.5 * (1.0 + t)
    return v * half, half + (0.5 * a) * v * (1.0 - t * t) * (1.0 + (3.0 * b) * sq)


def kernel(
    tok_in, w_in, hg_in, hid_out, ig_out, wg_out,
    tok, wbuf, hgb, s1, r1, s2, r2, zs, r3, tot, grad, hs, q, r8, r9, ws, acc, cs, cr,
    lr_send, lr_recv, ll_send, ll_recv, ig_buf, ig_bf,
    f_send, f_recv, w_loc, hg_loc, hid_loc, wg_loc, one_loc,
    t_recv, t_send, tc_recv, tc_send, c_send, c_recv, lr_ss, lr_rs, ll_ss, ll_rs,
):
    inp, l, dep = lax.axis_index("inp"), lax.axis_index("out"), lax.axis_index("dep")
    h, x = inp // NX, inp % NX
    y, c = dep // 2, dep % 2
    o = 1 - c

    def dev(h_=h, x_=x, l_=l, y_=y, c_=c):
        return (h_ * NX + x_, l_, y_ * 2 + c_)

    x_up, x_dn, x_far = (x + 1) % NX, (x + 3) % NX, (x + 2) % NX
    y_up, y_dn, y_far = (y + 1) % NY, (y + 3) % NY, (y + 2) % NY
    d_xu, d_xd, d_yu, d_yd = dev(x_=x_up), dev(x_=x_dn), dev(y_=y_up), dev(y_=y_dn)
    d_c, d_z = dev(c_=o), dev(h_=1 - h)
    zpos = h * NL + l
    zu, zd = (zpos + 1) % (2 * NL), (zpos + 2 * NL - 1) % (2 * NL)
    d_zu, d_zd = dev(h_=zu // NL, l_=zu % NL), dev(h_=zd // NL, l_=zd % NL)

    def rc(src, dst, ss, rs, to):
        return pltpu.make_async_remote_copy(
            src_ref=src, dst_ref=dst, send_sem=ss, recv_sem=rs, device_id=to, device_id_type=MESH
        )

    def cols(k, which):
        return pl.ds(pl.multiple_of(which * HALF + k * C, C), C)

    def w_rows(who):
        return pl.ds(pl.multiple_of(who * ROWS, 16), ROWS)

    top, bottom = pl.ds(0, ROWS), pl.ds(ROWS, ROWS)
    table = {
        "w_core": (lambda k: w_in.at[:, cols(k, o)], lambda k: wbuf.at[k, y, w_rows(c)],
                   d_c, lambda k: wbuf.at[k, y, w_rows(o)]),
        "w_up": (lambda k: wbuf.at[k, y], lambda k: wbuf.at[k, y], d_yu, lambda k: wbuf.at[k, y_dn]),
        "w_down": (lambda k: wbuf.at[k, y], lambda k: wbuf.at[k, y], d_yd, lambda k: wbuf.at[k, y_up]),
        "w_up2": (lambda k: wbuf.at[k, y_dn, top], lambda k: wbuf.at[k, y_dn, top],
                  d_yu, lambda k: wbuf.at[k, y_far, top]),
        "w_down2": (lambda k: wbuf.at[k, y_up, bottom], lambda k: wbuf.at[k, y_up, bottom],
                    d_yd, lambda k: wbuf.at[k, y_far, bottom]),
        "hg_core": (lambda k: hg_in.at[:, cols(k, o)], lambda k: hgb.at[k, c],
                    d_c, lambda k: hgb.at[k, o]),
        "s1_up": (lambda k: s1.at[k, 0], lambda k: r1.at[k, 0], d_xu, lambda k: r1.at[k, 0]),
        "s1_down": (lambda k: s1.at[k, 1], lambda k: r1.at[k, 1], d_xd, lambda k: r1.at[k, 1]),
        "s2_up": (lambda k: s2.at[k, 0], lambda k: r2.at[k, 0], d_xu, lambda k: r2.at[k, 0]),
        "s2_down": (lambda k: s2.at[k, 1], lambda k: r2.at[k, 1], d_xd, lambda k: r2.at[k, 1]),
        "z_pre": (lambda k: zs.at[k], lambda k: r3.at[k], d_z, lambda k: r3.at[k]),
        "z_grad": (lambda k: grad.at[k, x, h], lambda k: grad.at[k, x, h],
                   d_z, lambda k: grad.at[k, x, 1 - h]),
        "g_up": (lambda k: grad.at[k, x], lambda k: grad.at[k, x], d_xu, lambda k: grad.at[k, x_dn]),
        "g_down": (lambda k: grad.at[k, x], lambda k: grad.at[k, x], d_xd, lambda k: grad.at[k, x_up]),
        "g_up2": (lambda k: grad.at[k, x_dn, 0], lambda k: grad.at[k, x_dn, 0],
                  d_xu, lambda k: grad.at[k, x_far, 0]),
        "g_down2": (lambda k: grad.at[k, x_up, 1], lambda k: grad.at[k, x_up, 1],
                    d_xd, lambda k: grad.at[k, x_far, 1]),
        "hid_core": (lambda k: hs.at[k, o], lambda k: hid_out.at[:, cols(k, c)],
                     d_c, lambda k: hid_out.at[:, cols(k, o)]),
        "q1_up": (lambda k: q.at[k, y_far, top], lambda k: r8.at[k, 0], d_yu, lambda k: r8.at[k, 0]),
        "q1_down": (lambda k: q.at[k, y_far, bottom], lambda k: r8.at[k, 1], d_yd, lambda k: r8.at[k, 1]),
        "q2_up": (lambda k: q.at[k, y_up], lambda k: r9.at[k, 0], d_yu, lambda k: r9.at[k, 0]),
        "q2_down": (lambda k: q.at[k, y_dn], lambda k: r9.at[k, 1], d_yd, lambda k: r9.at[k, 1]),
        "wg_core": (lambda k: ws.at[k, o], lambda k: wg_out.at[:, cols(k, c)],
                    d_c, lambda k: wg_out.at[:, cols(k, o)]),
    }

    def desc(name, k):
        src, dst, to, _ = table[name]
        i = FLOWS.index(name)
        return rc(src(k), dst(k), f_send.at[i, k % SLOTS], f_recv.at[i, k], to)

    def when(cond, body):
        if isinstance(cond, bool):
            if cond:
                body()
        else:
            pl.when(cond)(body)

    def start(name, k):
        when(k >= SLOTS, lambda: desc(name, k - SLOTS).wait_send())
        desc(name, k).start()

    def arrived(name, k):
        src, _, to, got = table[name]
        i = FLOWS.index(name)
        rc(src(k), got(k), f_send.at[i, k % SLOTS], f_recv.at[i, k], to).wait_recv()

    barrier = pltpu.get_barrier_semaphore()
    friends = (d_xu, d_xd, d_yu, d_yd, d_c, d_z, d_zu, d_zd)
    for d in friends:
        pl.semaphore_signal(barrier, inc=1, device_id=d, device_id_type=MESH)

    def w_local(k):
        return pltpu.make_async_copy(w_in.at[:, cols(k, c)], wbuf.at[k, y, w_rows(c)], w_loc.at[k])

    def hg_local(k):
        return pltpu.make_async_copy(hg_in.at[:, cols(k, c)], hgb.at[k, c], hg_loc.at[k])

    def hid_local(k):
        return pltpu.make_async_copy(hs.at[k, c], hid_out.at[:, cols(k, c)], hid_loc.at[k])

    def wg_local(k):
        return pltpu.make_async_copy(ws.at[k, c], wg_out.at[:, cols(k, c)], wg_loc.at[k])

    def spot(ref, b, g):
        return ref.at[pl.ds(2 * (b % 2), 2), b // 2, g]

    own_tok = pltpu.make_async_copy(tok_in, spot(tok, l, c), one_loc.at[0])
    own_tok.start()

    @pl.loop(0, NC)
    def _(k):
        w_local(k).start()

    pl.semaphore_wait(barrier, len(friends))

    def tok_z(j, hh, way):
        return rc(tok.at[j, hh, c], tok.at[j, hh, c], t_send.at[way, j, hh], t_recv.at[j, hh],
                  d_zu if way == 0 else d_zd)

    def tok_c(j, hh, g):
        return rc(tok.at[j, hh, g], tok.at[j, hh, g], tc_send.at[j, hh], tc_recv.at[j, hh], d_c)

    def tok_step(j, step):
        for hh in range(2):
            b = j // 2 + 2 * hh

            def right():
                tok_z(j, hh, 0).start()

            def left():
                tok_z(j, hh, 1).start()

            def pass_on(ways):
                if step > 0:
                    tok_z(j, hh, 0).wait_recv()
                for cond, send in ways:
                    pl.when(cond)(send)
                tok_c(j, hh, c).start()

            if step == 0:
                pl.when(l == b)(lambda: pass_on(((l < NL - 1, right), (l > 0, left))))
            else:
                pl.when(l == b + step)(lambda: pass_on(((l < NL - 1, right),)))
                pl.when(l == b - step)(lambda: pass_on(((l > 0, left),)))

    def tok_ready(j):
        for hh in range(2):
            tok_c(j, hh, 1 - c).wait_recv()

    def dot_pre(j, k):
        rows = tok[j].reshape(4 * SUB, D)
        return jnp.dot(rows, wbuf[k].reshape(D, C), preferred_element_type=F32)

    def add_input(j, k):
        acc[j] += lax.dot_general(
            grad[k, j].reshape(4 * SUB, C), wbuf[k].reshape(D, C), (((1,), (1,)), ((), ())),
            preferred_element_type=F32,
        )

    def w_a(k):
        w_local(k).wait()
        arrived("w_core", k)
        start("w_up", k)
        start("w_down", k)

    def w_b(k):
        arrived("w_up", k)
        start("w_up2", k)
        arrived("w_down", k)
        start("w_down2", k)

    def pre1(k):
        arrived("w_up2", k)
        arrived("w_down2", k)
        s1[k] = dot_pre(x_far, k).astype(BF).reshape(2, 2 * SUB, C)
        start("s1_up", k)
        start("s1_down", k)
        hg_local(k).start()
        start("hg_core", k)

    def pre2(k):
        out = dot_pre(x_up, k).reshape(2, 2 * SUB, C)
        arrived("s1_up", k)
        s2[k, 0, 0] = (out[0] + r1[k, 0].astype(F32)).astype(BF)
        s2[k, 0, 1] = out[1].astype(BF)
        start("s2_up", k)
        out = dot_pre(x_dn, k).reshape(2, 2 * SUB, C)
        arrived("s1_down", k)
        s2[k, 1, 0] = out[0].astype(BF)
        s2[k, 1, 1] = (out[1] + r1[k, 1].astype(F32)).astype(BF)
        start("s2_down", k)

    def pre3(k):
        out = dot_pre(x, k).reshape(2, 2 * SUB, C)
        arrived("s2_up", k)
        arrived("s2_down", k)
        tot[k] = out + r2[k, 0].astype(F32) + r2[k, 1].astype(F32)
        zs[k] = tot[k, 1 - h].astype(BF)
        start("z_pre", k)

    def s4(k):
        hg_local(k).wait()
        arrived("hg_core", k)
        arrived("z_pre", k)
        v = tot[k, h] + r3[k].astype(F32)
        hidden, slope = act_and_slope(v)
        gp = hgb[k].reshape(2 * SUB, C).astype(F32) * slope
        grad[k, x, h] = gp.astype(BF)
        start("z_grad", k)
        hs[k] = hidden.astype(BF).reshape(2, SUB, C)
        hid_local(k).start()
        start("hid_core", k)

    def s5(k):
        arrived("z_grad", k)
        start("g_up", k)
        start("g_down", k)
        add_input(x, k)

    def s6(k):
        arrived("g_up", k)
        start("g_up2", k)
        arrived("g_down", k)
        start("g_down2", k)
        add_input(x_up, k)
        add_input(x_dn, k)

    def s7(k):
        arrived("g_up2", k)
        arrived("g_down2", k)
        add_input(x_far, k)
        out = lax.dot_general(
            tok[...].reshape(16 * SUB, D), grad[k].reshape(16 * SUB, C), (((0,), (0,)), ((), ())),
            preferred_element_type=F32,
        )
        q[k] = out.astype(BF).reshape(NY, 2 * ROWS, C)
        start("q1_up", k)
        start("q1_down", k)

    def q2(k):
        arrived("q1_up", k)
        q[k, y_up, top] = (q[k, y_up, top].astype(F32) + r8[k, 0].astype(F32)).astype(BF)
        start("q2_up", k)
        arrived("q1_down", k)
        q[k, y_dn, bottom] = (q[k, y_dn, bottom].astype(F32) + r8[k, 1].astype(F32)).astype(BF)
        start("q2_down", k)

    def q3(k):
        arrived("q2_up", k)
        arrived("q2_down", k)
        t = q[k, y].astype(F32) + r9[k, 0].astype(F32) + r9[k, 1].astype(F32)
        ws[k] = t.astype(BF).reshape(2, ROWS, C)
        wg_local(k).start()
        start("wg_core", k)

    stages = dict(w_a=w_a, w_b=w_b, pre1=pre1, pre2=pre2, pre3=pre3, s4=s4, s5=s5, s6=s6, s7=s7,
                  q2=q2, q3=q3)
    offset = dict(ORDER)

    def run(i, after=None):
        for name, off in ORDER:
            k = i - off
            body = stages[name]
            if isinstance(k, int):
                if 0 <= k < NC:
                    body(k)
                    if after is not None and k == NC - 1 and name in after:
                        after[name]()
            else:
                pl.when((k >= 0) & (k < NC))(functools.partial(body, k))

    sums = acc.reshape(NX, 2, 2, SUB, D)

    def to_core(j):
        return rc(cs.at[j], cr.at[j], c_send.at[j], c_recv.at[j], d_c)

    def ig_give(j):
        for hh in range(2):
            cs[j, hh] = sums[j, hh, o].astype(BF)
        to_core(j).start()

    def mine(j, hh):
        return sums[j, hh, c] + cr[j, hh].astype(F32)

    def line(j, hh, way):
        if way == 0:
            return rc(lr_send.at[j, hh], lr_recv.at[j, hh], lr_ss.at[j, hh], lr_rs.at[j, hh], d_zu)
        return rc(ll_send.at[j, hh], ll_recv.at[j, hh], ll_ss.at[j, hh], ll_rs.at[j, hh], d_zd)

    def ig_step(j, step):
        if step == 0:
            to_core(j).wait_recv()
        for hh in range(2):
            b = j // 2 + 2 * hh

            def move(way):
                out_buf, in_buf = (lr_send, lr_recv) if way == 0 else (ll_send, ll_recv)
                t = mine(j, hh)
                if step > 0:
                    line(j, hh, way).wait_recv()
                    t = t + in_buf[j, hh].astype(F32)
                out_buf[j, hh] = t.astype(BF)
                line(j, hh, way).start()

            pl.when((l == step) & (b > l))(functools.partial(move, 0))
            pl.when((l == NL - 1 - step) & (b < l))(functools.partial(move, 1))

    def ig_end(j):
        for hh in range(2):
            b = j // 2 + 2 * hh

            @pl.when(l == b)
            def _():
                spot_ = j % 2
                ig_buf[spot_] = mine(j, hh)

                @pl.when(l > 0)
                def _():
                    line(j, hh, 0).wait_recv()
                    ig_buf[spot_] += lr_recv[j, hh].astype(F32)

                @pl.when(l < NL - 1)
                def _():
                    line(j, hh, 1).wait_recv()
                    ig_buf[spot_] += ll_recv[j, hh].astype(F32)

                ig_bf[spot_] = ig_buf[spot_].astype(BF)

    own_tok.wait()
    start("w_core", 0)
    tok_step(x_far, 0)
    w_a(0)
    for k in range(1, SLOTS):
        start("w_core", k)
    tok_step(x_up, 0)
    w_a(1)
    tok_step(x_far, 1)
    tok_step(x_dn, 0)
    w_b(0)
    tok_step(x_up, 1)
    tok_step(x_far, 2)
    tok_step(x, 0)

    @pl.loop(SLOTS, NC)
    def _(k):
        start("w_core", k)

    acc[...] = jnp.zeros_like(acc)
    tok_step(x_dn, 1)
    tok_step(x_up, 2)
    w_b(1)
    w_a(2)
    tok_step(x_far, 3)
    tok_ready(x_far)
    run(0)
    tok_step(x, 1)
    tok_step(x_dn, 2)
    tok_step(x_up, 3)
    run(1)
    tok_step(x, 2)
    tok_step(x_dn, 3)
    tok_step(x, 3)
    tok_ready(x_up)
    tok_ready(x_dn)
    tok_ready(x)

    first_end = offset["s5"] + NC - 1
    pl.loop(2, first_end)(run)

    def after_s6():
        ig_step(x, 0)
        ig_give(x_up)
        ig_give(x_dn)
        ig_step(x, 1)

    def after_s7():
        ig_give(x_far)
        ig_step(x_up, 0)
        ig_step(x_dn, 0)
        ig_step(x, 2)
        ig_step(x_far, 0)
        ig_step(x_up, 1)
        ig_step(x_dn, 1)

    def after_q2():
        ig_step(x_far, 1)
        ig_step(x_up, 2)
        ig_step(x_dn, 2)
        ig_step(x_far, 2)

    after = {"s5": lambda: ig_give(x), "s6": after_s6, "s7": after_s7, "q2": after_q2}
    for i in range(first_end, offset["q3"] + NC):
        run(i, after)
    for j in (x, x_up, x_dn, x_far):
        ig_end(j)
    out_ig = pltpu.make_async_copy(ig_bf, ig_out, one_loc.at[0])
    out_ig.start()

    for name in FLOWS:
        for k in range(NC - SLOTS, NC):
            desc(name, k).wait_send()

    @pl.loop(0, NC)
    def _(k):
        arrived("hid_core", k)
        arrived("wg_core", k)
        hid_local(k).wait()
        wg_local(k).wait()

    for j in range(NX):
        for hh in range(2):
            b = j // 2 + 2 * hh
            pl.when((l >= b) & (l < NL - 1))(lambda: tok_z(j, hh, 0).wait_send())
            pl.when((l <= b) & (l > 0))(lambda: tok_z(j, hh, 1).wait_send())
            tok_c(j, hh, c).wait_send()
            pl.when(l < b)(lambda: line(j, hh, 0).wait_send())
            pl.when(l > b)(lambda: line(j, hh, 1).wait_send())
        to_core(j).wait_send()
    out_ig.wait()


def finish_kernel(hid_in, ig_in, wg_in, hid_out, ig_out, wg_out, hid, ig, half, full, in_sems, out_sems):
    rows = ROWS // PARTS

    def load(p):
        return pltpu.make_async_copy(wg_in.at[pl.ds(p * rows, rows)], half.at[p], in_sems.at[p])

    def store(p):
        return pltpu.make_async_copy(full.at[p], wg_out.at[pl.ds(p * rows, rows)], out_sems.at[p])

    through = (
        (pltpu.make_async_copy(hid_in, hid, in_sems.at[PARTS]),
         pltpu.make_async_copy(hid, hid_out, out_sems.at[PARTS])),
        (pltpu.make_async_copy(ig_in, ig, in_sems.at[PARTS + 1]),
         pltpu.make_async_copy(ig, ig_out, out_sems.at[PARTS + 1])),
    )
    for p in range(PARTS):
        load(p).start()
    for come, _ in through:
        come.start()
    for p in range(PARTS):
        load(p).wait()
        full[p] = half[p].astype(F32) * (1.0 / math.sqrt(TOKENS))
        store(p).start()
    for come, go in through:
        come.wait()
        go.start()
    for p in range(PARTS):
        store(p).wait()
    for _, go in through:
        go.wait()


def on_device(tokens, up_weight, hidden_grad):
    hbm = pl.BlockSpec(memory_space=pl.ANY)
    nf = len(FLOWS)
    dma = pltpu.SemaphoreType.DMA
    hidden, ig, wg = pl.pallas_call(
        kernel,
        out_shape=(
            jax.ShapeDtypeStruct((SUB, 2 * HALF), BF),
            jax.ShapeDtypeStruct((2, SUB, D), BF),
            jax.ShapeDtypeStruct((ROWS, 2 * HALF), BF),
        ),
        in_specs=[hbm] * 3,
        out_specs=[hbm] * 3,
        scratch_shapes=[
            pltpu.VMEM((NX, 2, 2, SUB, D), BF),
            pltpu.VMEM((NC, NY, 2 * ROWS, C), BF),
            pltpu.VMEM((NC, 2, SUB, C), BF),
            pltpu.VMEM((NC, 2, 2 * SUB, C), BF),
            pltpu.VMEM((NC, 2, 2 * SUB, C), BF),
            pltpu.VMEM((NC, 2, 2, 2 * SUB, C), BF),
            pltpu.VMEM((NC, 2, 2, 2 * SUB, C), BF),
            pltpu.VMEM((NC, 2 * SUB, C), BF),
            pltpu.VMEM((NC, 2 * SUB, C), BF),
            pltpu.VMEM((NC, 2, 2 * SUB, C), F32),
            pltpu.VMEM((NC, NX, 2, 2 * SUB, C), BF),
            pltpu.VMEM((NC, 2, SUB, C), BF),
            pltpu.VMEM((NC, NY, 2 * ROWS, C), BF),
            pltpu.VMEM((NC, 2, ROWS, C), BF),
            pltpu.VMEM((NC, 2, 2 * ROWS, C), BF),
            pltpu.VMEM((NC, 2, ROWS, C), BF),
            pltpu.VMEM((NX, 4 * SUB, D), F32),
            pltpu.VMEM((NX, 2, SUB, D), BF),
            pltpu.VMEM((NX, 2, SUB, D), BF),
            pltpu.VMEM((NX, 2, SUB, D), BF),
            pltpu.VMEM((NX, 2, SUB, D), BF),
            pltpu.VMEM((NX, 2, SUB, D), BF),
            pltpu.VMEM((NX, 2, SUB, D), BF),
            pltpu.VMEM((2, SUB, D), F32),
            pltpu.VMEM((2, SUB, D), BF),
            dma((nf, SLOTS)), dma((nf, NC)),
            dma((NC,)), dma((NC,)), dma((NC,)), dma((NC,)), dma((1,)),
            dma((NX, 2)), dma((2, NX, 2)), dma((NX, 2)), dma((NX, 2)), dma((NX,)), dma((NX,)),
            dma((NX, 2)), dma((NX, 2)), dma((NX, 2)), dma((NX, 2)),
        ],
        name="block",
        compiler_params=pltpu.CompilerParams(
            collective_id=0, has_side_effects=True, vmem_limit_bytes=62 << 20
        ),
    )(tokens.reshape(2, SUB, D), up_weight, hidden_grad)
    hidden, ig, wg = pl.pallas_call(
        finish_kernel,
        out_shape=(
            jax.ShapeDtypeStruct((SUB, 2 * HALF), BF),
            jax.ShapeDtypeStruct((2, SUB, D), BF),
            jax.ShapeDtypeStruct((ROWS, 2 * HALF), F32),
        ),
        in_specs=[hbm] * 3,
        out_specs=[hbm] * 3,
        scratch_shapes=[
            pltpu.VMEM((SUB, 2 * HALF), BF),
            pltpu.VMEM((2, SUB, D), BF),
            pltpu.VMEM((PARTS, ROWS // PARTS, 2 * HALF), BF),
            pltpu.VMEM((PARTS, ROWS // PARTS, 2 * HALF), F32),
            dma((PARTS + 2,)), dma((PARTS + 2,)),
        ],
        name="finish",
        compiler_params=pltpu.CompilerParams(vmem_limit_bytes=62 << 20),
    )(hidden, ig, wg)
    return hidden, ig.reshape(2 * SUB, D), wg


def solution(mesh):
    placed = (P(("dep", "out"), "inp"), P(("inp", "dep"), "out"), P(("dep", "inp"), "out"))
    return jax.shard_map(
        on_device,
        mesh=mesh,
        in_specs=placed,
        out_specs=(P(("dep", "inp"), "out"), P(("dep", "out"), "inp"), P(("inp", "dep"), "out")),
        check_vma=False,
    )
```
